32 devices in a mesh: half: 2 (over core), row: 8 (over z, x), col: 2 (over y).
Axes of the slice: x: 2, y: 2, z: 4, core: 2. Of those that a mesh axis runs over, the one named last changes fastest.
Arguments:
- front_matrix: bfloat16 [16384, 2, 2, 4096], P('row', 'col', 'half'), may hold values from -6 to 6
- child_update: bfloat16 [2, 12288, 12288], P('half', 'row', 'col'), may hold values from -6 to 6
- fill_pattern: int32 [2, 96, 96], replicated, may hold values 0 or 1
- child_map: int32 [2, 96], replicated, may hold values from 0 to 127, as said below
- first_inverse: bfloat16 [256, 256], replicated, as said below
- second_inverse: bfloat16 [256, 256], replicated, as said below
Outputs:
- factored: bfloat16 [16384, 2, 2, 4096], P('row', 'col', 'half')
The draws below stay inside these ranges and needn't reach their ends.
Inputs may be any that keep to these rules, and one draw needn't show every extreme that they name: `child_map`: child block i of each child maps to front block 4 * (i // 3) + t with t in 0 to 3, rising with i inside each group of three; the first child block maps to front block 0 and the last to front block 127. `first_inverse`: entries lie within 1/128 of zero. `second_inverse`: entries lie within 1/128 of zero.
All inputs are finite; a program needn't handle non-finite values.
Results may differ from the reference program's by a relative error of at most 0.002.
Values may be sent and summed in bfloat16 or wider, within the bound.
A program may use at most 256 MiB of HBM per device.

```python
import jax
import jax.numpy as jnp
from jax import lax

FRONT = 16384
BLOCK = 128
PANEL = 256
CHILD = 12288
CHILD_BLOCKS = 96
SLAB = 4096
N_COL = 2


def draw_child_map(key, part):
    key = jax.random.fold_in(key, 7)
    count = 3 * FRONT // (4 * BLOCK)
    groups = count // 3
    key_mid, key_first, key_last = jax.random.split(key, 3)
    dropped = jax.random.randint(key_mid, (2, groups), 0, 4)
    dropped = dropped.at[:, 0].set(jax.random.randint(key_first, (2,), 1, 4))
    dropped = dropped.at[:, groups - 1].set(jax.random.randint(key_last, (2,), 0, 3))
    within = jnp.arange(count, dtype=jnp.int32) % 3
    group_of = jnp.arange(count, dtype=jnp.int32) // 3
    gap = dropped[:, group_of]
    mapped = 4 * group_of[None, :] + within[None, :] + (within[None, :] >= gap).astype(jnp.int32)
    return mapped.astype(jnp.int32)


def signed_flat(key):
    key_rows, key_cols = jax.random.split(key)
    positions = jnp.arange(PANEL, dtype=jnp.int32)
    crossed = jnp.bitwise_and(positions[:, None], positions[None, :])
    parity = jnp.zeros((PANEL, PANEL), jnp.int32)
    for bit_level in range(PANEL.bit_length()):
        parity = parity + crossed // 2 ** bit_level % 2
    pattern = 1 - 2 * (parity % 2)
    row_signs = 2 * jax.random.randint(key_rows, (PANEL,), 0, 2) - 1
    col_signs = 2 * jax.random.randint(key_cols, (PANEL,), 0, 2) - 1
    values = (pattern * row_signs[:, None] * col_signs[None, :]).astype(jnp.float32) * (1.0 / 128.0)
    return values.astype(jnp.bfloat16)


def draw_first_inverse(key, part):
    key = jax.random.fold_in(key, 11)
    return signed_flat(key)


def draw_second_inverse(key, part):
    key = jax.random.fold_in(key, 13)
    return signed_flat(key)


def with_ends(entries, key, least, top_value):
    longest = entries.shape.index(max(entries.shape))
    spots = []
    for shift in (0, 1):
        where = [jax.random.randint(jax.random.fold_in(key, axis), (), 0, length) for axis, length in enumerate(entries.shape)]
        where[longest] = (where[longest] + shift) % entries.shape[longest]
        spots.append(tuple(where))
    return entries.at[spots[0]].set(least).at[spots[1]].set(top_value)


def block_scale(own_key, shape, pieces, smallest, high):
    def one(dim, parts):
        heights = jax.random.uniform(jax.random.fold_in(jax.random.fold_in(own_key, 6), dim), (parts,), jnp.float32, smallest / len(pieces), high / len(pieces))
        return jnp.repeat(jnp.exp(heights), shape[dim] // parts).reshape((-1,) + (1,) * (len(shape) - dim - 1))

    gain = one(*pieces[0])
    for cut in pieces[1:]:
        gain = gain * one(*cut)
    return gain


def noise(stream_key, shape, spread, bound, cuts=(), kind=jnp.bfloat16):
    level = block_scale(stream_key, shape, cuts, -0.22, 0.18) if cuts else 1.0
    result = jax.random.normal(stream_key, shape, jnp.float32) * spread * level
    return jnp.minimum(jnp.maximum(result, -bound), bound).astype(kind)


def setup_inputs(seed: int = 0) -> dict:
    key_of = jax.random.split(jax.random.key(seed), 7)
    front_matrix = noise(key_of[0], (FRONT, N_COL, 2, SLAB), 1.0, 6.0, ((0, 8), (1, 2), (2, 2)))
    child_update = noise(key_of[1], (2, CHILD, CHILD), 1.0, 6.0, ((0, 2), (1, 8), (2, 2)))
    fill_pattern = with_ends((jax.random.randint(key_of[2], (2, CHILD_BLOCKS, CHILD_BLOCKS), 0, 4) < 3).astype(jnp.int32), jax.random.fold_in(key_of[2], 1), 0, 1)
    child_map = draw_child_map(jax.random.fold_in(key_of[6], 71), 0)
    first_inverse = draw_first_inverse(jax.random.fold_in(key_of[6], 71), 0)
    second_inverse = draw_second_inverse(jax.random.fold_in(key_of[6], 71), 0)
    return dict(front_matrix=front_matrix, child_update=child_update, fill_pattern=fill_pattern, child_map=child_map, first_inverse=first_inverse, second_inverse=second_inverse)


def reference(front_matrix, child_update, fill_pattern, child_map, first_inverse, second_inverse):
    order = front_matrix.shape[0]
    shape_out = front_matrix.shape
    assembled = front_matrix.reshape(order, order).astype(jnp.float32)
    offsets = jnp.arange(BLOCK, dtype=jnp.int32)
    for source in range(2):
        positions = (child_map[source][:, None] * BLOCK + offsets[None, :]).reshape(-1).astype(jnp.int32)
        fill_full = jnp.repeat(jnp.repeat(fill_pattern[source], BLOCK, axis=0), BLOCK, axis=1).astype(jnp.float32)
        values = child_update[source].astype(jnp.float32) * fill_full
        assembled = assembled.at[positions[:, None], positions[None, :]].add(values)
    row_index = jnp.arange(order, dtype=jnp.int32)[:, None]
    first_raw = jnp.dot(assembled[:, :PANEL], first_inverse.astype(jnp.float32).T,
                        precision=lax.Precision.HIGHEST).astype(jnp.bfloat16)
    first_low = jnp.where(row_index >= PANEL, first_raw, jnp.zeros_like(first_raw))
    updated = assembled - jnp.dot(first_low, first_low.T, preferred_element_type=jnp.float32)
    second_full = jnp.dot(updated[:, PANEL:2 * PANEL], second_inverse.astype(jnp.float32).T,
                          precision=lax.Precision.HIGHEST)
    second_raw = jnp.where(row_index >= PANEL, second_full, jnp.zeros_like(second_full)).astype(jnp.bfloat16)
    second_low = jnp.where(row_index >= 2 * PANEL, second_raw, jnp.zeros_like(second_raw))
    final = updated - jnp.dot(second_low, second_low.T, preferred_element_type=jnp.float32)
    panels = jnp.concatenate([first_raw, second_raw], axis=1).astype(jnp.float32)
    final = jnp.concatenate([panels, final[:, 2 * PANEL:]], axis=1)
    return final.astype(jnp.bfloat16).reshape(shape_out)
```

```python
import functools

import jax
import jax.numpy as jnp
from jax import lax
from jax.experimental import pallas as pl
from jax.experimental.pallas import tpu as pltpu
from jax.sharding import PartitionSpec as P

BLOCK = 128
PANEL = 256
BOTH = 2 * PANEL
GROUP = 3 * BLOCK
CHUNKS = 4
MESH_IDS = pl.DeviceIdType.MESH
F32 = jnp.float32
BF16 = jnp.bfloat16


def dot_t(a, b):
    return lax.dot_general(a, b, (((1,), (1,)), ((), ())), preferred_element_type=F32)


def dot_exact(a, b):
    high = a.astype(BF16)
    rest = a - high.astype(F32)
    mid = rest.astype(BF16)
    low = (rest - mid.astype(F32)).astype(BF16)
    return dot_t(low, b) + dot_t(mid, b) + dot_t(high, b)


def locate(cmap, source, group, slot):
    target = 4 * group + slot
    m0 = cmap[source, 3 * group]
    m1 = cmap[source, 3 * group + 1]
    m2 = cmap[source, 3 * group + 2]
    k = jnp.where(m1 <= target, 1, 0)
    k = jnp.where(m2 <= target, 2, k)
    hit = (m0 == target) | (m1 == target) | (m2 == target)
    return k, hit


def panel_kernel(
    n_half, n_row, n_col,
    front, child, fill, cmap, inverse1, inverse2,
    received, lrows, lcols, raw,
    front_v, own_v, other_v, asm, l_v, raw_v, top_v,
    load_sem, early_send, early_recv, late_send, late_recv, top_send, top_recv,
    row_send, row_recv, line_send, line_recv, lane_send, lane_recv, out_sem,
):
    rows = front.shape[0]
    half_width = received.shape[1]
    chunk = rows // CHUNKS
    fanout = n_row // (2 * n_col)
    n_z = n_row // fanout
    h, r, c = lax.axis_index("half"), lax.axis_index("row"), lax.axis_index("col")
    slab = 2 * c + h
    z, lane = lax.div(r, fanout), lax.rem(r, fanout)
    root = slab == 0

    barrier = pltpu.get_barrier_semaphore()
    pl.semaphore_signal(barrier, inc=1, device_id={"half": 1 - h}, device_id_type=MESH_IDS)
    for k in range(1, n_col):
        pl.semaphore_signal(
            barrier, inc=1, device_id={"col": lax.rem(c + k, n_col)}, device_id_type=MESH_IDS
        )
    for k in range(1, n_row):
        pl.semaphore_signal(
            barrier, inc=1, device_id={"row": lax.rem(r + k, n_row)}, device_id_type=MESH_IDS
        )
    load_front = pltpu.make_async_copy(front.at[:, pl.ds(0, BOTH)], front_v, load_sem.at[0])
    load_own = pltpu.make_async_copy(child.at[:, pl.ds(0, GROUP)], own_v, load_sem.at[1])

    @pl.when(root)
    def _():
        load_front.start()
        load_own.start()

    pl.semaphore_wait(barrier, 1 + (n_col - 1) + (n_row - 1))

    early = pltpu.make_async_remote_copy(
        src_ref=child.at[:, pl.ds(0, GROUP)], dst_ref=other_v,
        send_sem=early_send, recv_sem=early_recv,
        device_id={"half": 1 - h}, device_id_type=MESH_IDS,
    )
    start = pl.multiple_of((1 - h) * half_width, 128)
    late = pltpu.make_async_remote_copy(
        src_ref=child.at[:, pl.ds(start, half_width)], dst_ref=received,
        send_sem=late_send, recv_sem=late_recv,
        device_id={"half": 1 - h}, device_id_type=MESH_IDS,
    )

    @pl.when(slab == 1)
    def _():
        early.start()

    late.start()

    def part(ref, k):
        return ref.at[pl.ds(k * chunk, chunk), :]

    def slot_part(ref, k):
        return ref.at[pl.ds(pl.multiple_of(lane * rows + k * chunk, chunk), chunk), :]

    def to_col(k, j):
        return pltpu.make_async_remote_copy(
            src_ref=part(l_v, k), dst_ref=part(lrows, k),
            send_sem=row_send.at[j, k], recv_sem=row_recv.at[k],
            device_id={"col": j}, device_id_type=MESH_IDS,
        )

    def to_half(k, src):
        return pltpu.make_async_remote_copy(
            src_ref=part(src, k), dst_ref=part(lrows, k),
            send_sem=row_send.at[0, k], recv_sem=row_recv.at[k],
            device_id={"half": 1 - h}, device_id_type=MESH_IDS,
        )

    def to_line(k, step, src):
        return pltpu.make_async_remote_copy(
            src_ref=src, dst_ref=slot_part(lcols, k),
            send_sem=line_send.at[(step + 1) // 2, k], recv_sem=line_recv.at[k],
            device_id={"row": r + step * fanout}, device_id_type=MESH_IDS,
        )

    def to_lane(k, d, src):
        return pltpu.make_async_remote_copy(
            src_ref=src, dst_ref=slot_part(lcols, k),
            send_sem=lane_send.at[d, k], recv_sem=lane_recv.at[d, k],
            device_id={"row": z * fanout + lax.rem(lane + d, fanout)}, device_id_type=MESH_IDS,
        )

    def keep_rows(k):
        return pltpu.make_async_copy(part(l_v, k), part(lrows, k), out_sem.at[0, k])

    def keep_raw(k):
        return pltpu.make_async_copy(part(raw_v, k), part(raw, k), out_sem.at[1, k])

    def keep_cols(k, src):
        return pltpu.make_async_copy(part(src, k), slot_part(lcols, k), out_sem.at[2, k])

    def send_cols(k, src, src_slot):
        @pl.when(z + 1 < n_z)
        def _():
            to_line(k, 1, part(src, k)).start()

        @pl.when(z >= 1)
        def _():
            to_line(k, -1, part(src, k)).start()

        for d in range(1, fanout):
            to_lane(k, d, part(src, k)).start()
        keep_cols(k, src).start()

    @pl.when(root)
    def _():
        load_front.wait()
        load_own.wait()
        early.wait_recv()
        groups = rows // BOTH

        def lands(source, index, target):
            apart = cmap[source, index] - target
            return 1 - jnp.minimum(apart * apart, 1)

        def assemble(g, carry):
            group = r * groups + g
            for t in range(4):
                row0 = pl.multiple_of(g * BOTH + t * BLOCK, BLOCK)
                for q in range(4):
                    total = front_v[pl.ds(row0, BLOCK), q * BLOCK : (q + 1) * BLOCK].astype(F32)
                    for source, piece in ((0, own_v), (1, other_v)):
                        for kr in range(max(t - 1, 0), min(t, 2) + 1):
                            hit_r = lands(source, 3 * group + kr, 4 * group + t)
                            for kc in range(max(q - 1, 0), min(q, 2) + 1):
                                hit = hit_r * lands(source, kc, q) * fill[source, 3 * group + kr, kc]
                                block = piece[
                                    pl.ds(pl.multiple_of(g * GROUP + kr * BLOCK, BLOCK), BLOCK),
                                    kc * BLOCK : (kc + 1) * BLOCK,
                                ]
                                total = total + block.astype(F32) * hit.astype(F32)
                    asm[pl.ds(row0, BLOCK), q * BLOCK : (q + 1) * BLOCK] = total
            return carry

        lax.fori_loop(0, groups, assemble, 0)

        step_rows = PANEL

        def first(k, carry):
            row0 = pl.multiple_of(k * step_rows, step_rows)
            value = dot_exact(asm[pl.ds(row0, step_rows), 0:PANEL], inverse1[...]).astype(BF16)
            raw_v[pl.ds(row0, step_rows), 0:PANEL] = value
            keep = r * rows + row0 >= PANEL
            l_v[pl.ds(row0, step_rows), 0:PANEL] = jnp.where(keep, value, jnp.zeros_like(value))
            return carry

        lax.fori_loop(0, rows // step_rows, first, 0)

        def to_top(j):
            return pltpu.make_async_remote_copy(
                src_ref=top_v, dst_ref=top_v, send_sem=top_send.at[j], recv_sem=top_recv,
                device_id={"row": j}, device_id_type=MESH_IDS,
            )

        @pl.when(r == 0)
        def _():
            top_v[...] = raw_v[PANEL:BOTH, 0:PANEL]
            for j in range(1, n_row):
                to_top(j).start()

        @pl.when(r != 0)
        def _():
            to_top(0).wait_recv()

        for k in range(CHUNKS):

            def second(i, carry):
                row0 = pl.multiple_of(k * chunk + i * step_rows, step_rows)
                here = pl.ds(row0, step_rows)
                updated = asm[here, PANEL:BOTH] - dot_t(l_v[here, 0:PANEL], top_v[...])
                value = dot_exact(updated, inverse2[...]).astype(BF16)
                none = jnp.zeros_like(value)
                raw_v[here, PANEL:BOTH] = jnp.where(r * rows + row0 >= PANEL, value, none)
                l_v[here, PANEL:BOTH] = jnp.where(r * rows + row0 >= BOTH, value, none)
                return carry

            lax.fori_loop(0, chunk // step_rows, second, 0)
            for j in range(1, n_col):
                to_col(k, j).start()
            to_half(k, l_v).start()
            keep_rows(k).start()
            keep_raw(k).start()

            @pl.when(z == slab)
            def _():
                send_cols(k, l_v, None)

        @pl.when(r == 0)
        def _():
            for j in range(1, n_row):
                to_top(j).wait_send()

    for k in range(CHUNKS):

        @pl.when(slab != 0)
        def _():
            to_half(k, lrows).wait_recv()

            @pl.when((h == 0) & (c != 0))
            def _():
                to_half(k, lrows).start()

            @pl.when(z == slab)
            def _():
                send_cols(k, lrows, None)

        @pl.when(z != slab)
        def _():
            here = slot_part(lcols, k)
            to_line(k, 1, here).wait_recv()

            @pl.when((z > slab) & (z + 1 < n_z))
            def _():
                to_line(k, 1, here).start()

            @pl.when((z < slab) & (z >= 1))
            def _():
                to_line(k, -1, here).start()

            for d in range(1, fanout):
                to_lane(k, d, here).start()

    for k in range(CHUNKS):
        here = slot_part(lcols, k)
        for d in range(1, fanout):
            other = lax.rem(lane + fanout - d, fanout)
            landed = lcols.at[pl.ds(pl.multiple_of(other * rows + k * chunk, chunk), chunk), :]
            pltpu.make_async_remote_copy(
                src_ref=landed, dst_ref=landed, send_sem=lane_send.at[d, k],
                recv_sem=lane_recv.at[d, k], device_id={"half": 1 - h}, device_id_type=MESH_IDS,
            ).wait_recv()
            to_lane(k, d, here).wait_send()

        @pl.when(root)
        def _():
            for j in range(1, n_col):
                to_col(k, j).wait_send()
            keep_rows(k).wait()
            keep_raw(k).wait()

        @pl.when(h == 0)
        def _():
            to_half(k, lrows).wait_send()

        @pl.when((z >= slab) & (z + 1 < n_z))
        def _():
            to_line(k, 1, here).wait_send()

        @pl.when((z <= slab) & (z >= 1))
        def _():
            to_line(k, -1, here).wait_send()

        @pl.when(z == slab)
        def _():
            keep_cols(k, lrows).wait()

    @pl.when(slab == 1)
    def _():
        early.wait_send()

    late.wait()


def update_kernel(
    place, cmap, fill, front, own, other, lrows, lcols, raw, out, product
):
    half, slab, row_group0, col_group0 = place[0], place[1], place[2], place[3]
    j, i = pl.program_id(0), pl.program_id(1)
    tile_cols = front.shape[1]
    product[...] = dot_t(lrows[...], lcols[...])
    row_group = row_group0 + i
    pieces = ((half, own), (1 - half, other))
    row_spots = [[locate(cmap, source, row_group, p) for p in range(4)] for source, _ in pieces]
    for q in range(tile_cols // BLOCK):
        col_group = col_group0 + j * (tile_cols // BOTH) + q // 4
        col_spots = [locate(cmap, source, col_group, q % 4) for source, _ in pieces]
        columns = slice(q * BLOCK, (q + 1) * BLOCK)
        for p in range(4):
            here = slice(p * BLOCK, (p + 1) * BLOCK)
            total = front[here, columns].astype(F32)
            for n, (source, piece) in enumerate(pieces):
                kr, hit_r = row_spots[n][p]
                kc, hit_c = col_spots[n]
                use = hit_r & hit_c & (fill[source, 3 * row_group + kr, 3 * col_group + kc] != 0)
                block = piece[
                    pl.ds(pl.multiple_of(kr * BLOCK, BLOCK), BLOCK),
                    pl.ds(pl.multiple_of(q // 4 * GROUP + kc * BLOCK, BLOCK), BLOCK),
                ]
                total = total + jnp.where(use, block.astype(F32), 0.0)
            out[here, columns] = (total - product[here, columns]).astype(BF16)

    @pl.when((slab == 0) & (j == 0))
    def _():
        out[:, 0:BOTH] = raw[...]


def body(sizes, front_matrix, child_update, fill_pattern, child_map, first_inverse, second_inverse):
    n_half, n_row, n_col = sizes
    rows, width = front_matrix.shape[0], front_matrix.shape[3]
    front = front_matrix.reshape(rows, width)
    child = child_update.reshape(child_update.shape[1:])
    child_rows, half_width = child.shape[0], child.shape[1] // 2
    fanout = n_row // (2 * n_col)
    any_space = pl.BlockSpec(memory_space=pl.ANY)
    smem = pl.BlockSpec(memory_space=pltpu.SMEM)
    vmem = pl.BlockSpec(memory_space=pltpu.VMEM)
    dma = pltpu.SemaphoreType.DMA
    received, lrows, lcols, raw = pl.pallas_call(
        functools.partial(panel_kernel, n_half, n_row, n_col),
        out_shape=[
            jax.ShapeDtypeStruct((child_rows, half_width), BF16),
            jax.ShapeDtypeStruct((rows, BOTH), BF16),
            jax.ShapeDtypeStruct((width, BOTH), BF16),
            jax.ShapeDtypeStruct((rows, BOTH), BF16),
        ],
        in_specs=[any_space, any_space, smem, smem, vmem, vmem],
        out_specs=[any_space] * 4,
        scratch_shapes=[
            pltpu.VMEM((rows, BOTH), BF16),
            pltpu.VMEM((child_rows, GROUP), BF16),
            pltpu.VMEM((child_rows, GROUP), BF16),
            pltpu.VMEM((rows, BOTH), F32),
            pltpu.VMEM((rows, BOTH), BF16),
            pltpu.VMEM((rows, BOTH), BF16),
            pltpu.VMEM((PANEL, PANEL), BF16),
            dma((2,)), dma, dma, dma, dma, dma((n_row,)), dma,
            dma((n_col, CHUNKS)), dma((CHUNKS,)),
            dma((2, CHUNKS)), dma((CHUNKS,)),
            dma((fanout, CHUNKS)), dma((fanout, CHUNKS)), dma((3, CHUNKS)),
        ],
        compiler_params=pltpu.CompilerParams(
            collective_id=0, has_side_effects=True, vmem_limit_bytes=40 * 2**20
        ),
        name="panels",
    )(front, child, fill_pattern, child_map, first_inverse, second_inverse)

    half = lax.axis_index("half")
    row = lax.axis_index("row")
    slab = lax.axis_index("col") * 2 + half
    place = jnp.stack([half, slab, row * (rows // BOTH), slab * (width // BOTH)]).astype(jnp.int32)
    tile = 2 * BOTH
    tile_child = 2 * GROUP
    halves = half_width // tile_child
    out = pl.pallas_call(
        update_kernel,
        out_shape=jax.ShapeDtypeStruct((rows, width), BF16),
        grid_spec=pltpu.PrefetchScalarGridSpec(
            num_scalar_prefetch=3,
            grid=(width // tile, rows // BOTH),
            in_specs=[
                pl.BlockSpec((BOTH, tile), lambda j, i, *_: (i, j)),
                pl.BlockSpec((GROUP, tile_child), lambda j, i, place, *_: (i, place[0] * halves + j)),
                pl.BlockSpec((GROUP, tile_child), lambda j, i, *_: (i, j)),
                pl.BlockSpec((BOTH, BOTH), lambda j, i, *_: (i, 0)),
                pl.BlockSpec((tile, BOTH), lambda j, i, *_: (j, 0)),
                pl.BlockSpec((BOTH, BOTH), lambda j, i, *_: (i, 0)),
            ],
            out_specs=pl.BlockSpec((BOTH, tile), lambda j, i, *_: (i, j)),
            scratch_shapes=[pltpu.VMEM((BOTH, tile), F32)],
        ),
        compiler_params=pltpu.CompilerParams(vmem_limit_bytes=48 * 2**20),
        name="update",
    )(place, child_map, fill_pattern, front, child, received, lrows, lcols, raw)
    return out.reshape(rows, 1, 1, width)


def solution(mesh):
    placed = (P("row", "col", "half", None), P("half", "row", "col"), P(), P(), P(), P())
    sizes = (mesh.shape["half"], mesh.shape["row"], mesh.shape["col"])
    return jax.shard_map(
        functools.partial(body, sizes), mesh=mesh, in_specs=placed,
        out_specs=P("row", "col", "half", None), check_vma=False,
    )
```

```python
import functools

import jax
import jax.numpy as jnp
from jax import lax
from jax.experimental import pallas as pl
from jax.experimental.pallas import tpu as pltpu
from jax.sharding import PartitionSpec as P

BLOCK = 128
PANEL = 256
BOTH = 2 * PANEL
GROUP = 3 * BLOCK
CHUNKS = 8
LAG = 3
MESH_IDS = pl.DeviceIdType.MESH
F32 = jnp.float32
BF16 = jnp.bfloat16


def dot_t(a, b):
    return lax.dot_general(a, b, (((1,), (1,)), ((), ())), preferred_element_type=F32)


def dot_exact(a, b):
    high = a.astype(BF16)
    rest = a - high.astype(F32)
    mid = rest.astype(BF16)
    low = (rest - mid.astype(F32)).astype(BF16)
    return dot_t(low, b) + dot_t(mid, b) + dot_t(high, b)


def locate(cmap, source, group, slot):
    target = 4 * group + slot
    m0 = cmap[source, 3 * group]
    m1 = cmap[source, 3 * group + 1]
    m2 = cmap[source, 3 * group + 2]
    k = jnp.where(m1 <= target, 1, 0)
    k = jnp.where(m2 <= target, 2, k)
    hit = (m0 == target) | (m1 == target) | (m2 == target)
    return k, hit


def panel_kernel(
    n_half, n_row, n_col,
    front, child, fill, cmap, inverse1, inverse2,
    received, lrows, lcols, raw,
    front_v, own_v, other_v, asm, l_v, raw_v, top_v,
    load_sem, early_send, early_recv, late_send, late_recv, top_send, top_recv,
    row_send, row_recv, line_send, line_recv, lane_send, lane_recv, out_sem,
):
    rows = front.shape[0]
    half_width = received.shape[1]
    chunk = rows // CHUNKS
    fanout = n_row // (2 * n_col)
    n_z = n_row // fanout
    h, r, c = lax.axis_index("half"), lax.axis_index("row"), lax.axis_index("col")
    slab = 2 * c + h
    z, lane = lax.div(r, fanout), lax.rem(r, fanout)
    root = slab == 0

    barrier = pltpu.get_barrier_semaphore()
    pl.semaphore_signal(barrier, inc=1, device_id={"half": 1 - h}, device_id_type=MESH_IDS)
    for k in range(1, n_col):
        pl.semaphore_signal(
            barrier, inc=1, device_id={"col": lax.rem(c + k, n_col)}, device_id_type=MESH_IDS
        )
    for k in range(1, n_row):
        pl.semaphore_signal(
            barrier, inc=1, device_id={"row": lax.rem(r + k, n_row)}, device_id_type=MESH_IDS
        )
    load_front = pltpu.make_async_copy(front.at[:, pl.ds(0, BOTH)], front_v, load_sem.at[0])
    load_own = pltpu.make_async_copy(child.at[:, pl.ds(0, GROUP)], own_v, load_sem.at[1])

    @pl.when(root)
    def _():
        load_front.start()
        load_own.start()

    pl.semaphore_wait(barrier, 1 + (n_col - 1) + (n_row - 1))

    early = pltpu.make_async_remote_copy(
        src_ref=child.at[:, pl.ds(0, GROUP)], dst_ref=other_v,
        send_sem=early_send, recv_sem=early_recv,
        device_id={"half": 1 - h}, device_id_type=MESH_IDS,
    )
    start = pl.multiple_of((1 - h) * half_width, 128)
    late = pltpu.make_async_remote_copy(
        src_ref=child.at[:, pl.ds(start, half_width)], dst_ref=received,
        send_sem=late_send, recv_sem=late_recv,
        device_id={"half": 1 - h}, device_id_type=MESH_IDS,
    )

    @pl.when(slab == 1)
    def _():
        early.start()

    late.start()

    def part(ref, k):
        return ref.at[pl.ds(k * chunk, chunk), :]

    def slot_part(ref, k):
        return ref.at[pl.ds(pl.multiple_of(lane * rows + k * chunk, chunk), chunk), :]

    def to_col(k, j):
        return pltpu.make_async_remote_copy(
            src_ref=part(l_v, k), dst_ref=part(lrows, k),
            send_sem=row_send.at[j, k], recv_sem=row_recv.at[k],
            device_id={"col": j}, device_id_type=MESH_IDS,
        )

    def to_half(k, src):
        return pltpu.make_async_remote_copy(
            src_ref=part(src, k), dst_ref=part(lrows, k),
            send_sem=row_send.at[0, k], recv_sem=row_recv.at[k],
            device_id={"half": 1 - h}, device_id_type=MESH_IDS,
        )

    def to_line(k, step, src):
        return pltpu.make_async_remote_copy(
            src_ref=src, dst_ref=slot_part(lcols, k),
            send_sem=line_send.at[(step + 1) // 2, k], recv_sem=line_recv.at[k],
            device_id={"row": r + step * fanout}, device_id_type=MESH_IDS,
        )

    def to_lane(k, d, src):
        return pltpu.make_async_remote_copy(
            src_ref=src, dst_ref=slot_part(lcols, k),
            send_sem=lane_send.at[d, k], recv_sem=lane_recv.at[d, k],
            device_id={"row": z * fanout + lax.rem(lane + d, fanout)}, device_id_type=MESH_IDS,
        )

    def keep_rows(k):
        return pltpu.make_async_copy(part(l_v, k), part(lrows, k), out_sem.at[0, k])

    def keep_raw(k):
        return pltpu.make_async_copy(part(raw_v, k), part(raw, k), out_sem.at[1, k])

    def keep_cols(k, src):
        return pltpu.make_async_copy(part(src, k), slot_part(lcols, k), out_sem.at[2, k])

    def send_cols(k, src, src_slot):
        @pl.when(z + 1 < n_z)
        def _():
            to_line(k, 1, part(src, k)).start()

        @pl.when(z >= 1)
        def _():
            to_line(k, -1, part(src, k)).start()

        for d in range(1, fanout):
            to_lane(k, d, part(src, k)).start()
        keep_cols(k, src).start()

    @pl.when(root)
    def _():
        load_front.wait()
        load_own.wait()
        early.wait_recv()
        groups = rows // BOTH

        def lands(source, index, target):
            apart = cmap[source, index] - target
            return 1 - jnp.minimum(apart * apart, 1)

        def assemble(g, carry):
            group = r * groups + g
            for t in range(4):
                row0 = pl.multiple_of(g * BOTH + t * BLOCK, BLOCK)
                for q in range(4):
                    total = front_v[pl.ds(row0, BLOCK), q * BLOCK : (q + 1) * BLOCK].astype(F32)
                    for source, piece in ((0, own_v), (1, other_v)):
                        for kr in range(max(t - 1, 0), min(t, 2) + 1):
                            hit_r = lands(source, 3 * group + kr, 4 * group + t)
                            for kc in range(max(q - 1, 0), min(q, 2) + 1):
                                hit = hit_r * lands(source, kc, q) * fill[source, 3 * group + kr, kc]
                                block = piece[
                                    pl.ds(pl.multiple_of(g * GROUP + kr * BLOCK, BLOCK), BLOCK),
                                    kc * BLOCK : (kc + 1) * BLOCK,
                                ]
                                total = total + block.astype(F32) * hit.astype(F32)
                    asm[pl.ds(row0, BLOCK), q * BLOCK : (q + 1) * BLOCK] = total
            return carry

        lax.fori_loop(0, groups, assemble, 0)

        step_rows = PANEL

        def first(k, carry):
            row0 = pl.multiple_of(k * step_rows, step_rows)
            value = dot_exact(asm[pl.ds(row0, step_rows), 0:PANEL], inverse1[...]).astype(BF16)
            raw_v[pl.ds(row0, step_rows), 0:PANEL] = value
            keep = r * rows + row0 >= PANEL
            l_v[pl.ds(row0, step_rows), 0:PANEL] = jnp.where(keep, value, jnp.zeros_like(value))
            return carry

        lax.fori_loop(0, rows // step_rows, first, 0)

        def to_top(j):
            return pltpu.make_async_remote_copy(
                src_ref=top_v, dst_ref=top_v, send_sem=top_send.at[j], recv_sem=top_recv,
                device_id={"row": j}, device_id_type=MESH_IDS,
            )

        @pl.when(r == 0)
        def _():
            top_v[...] = raw_v[PANEL:BOTH, 0:PANEL]
            for j in range(1, n_row):
                to_top(j).start()

        @pl.when(r != 0)
        def _():
            to_top(0).wait_recv()

        short_rows = min(PANEL, chunk)
        for k in range(CHUNKS):

            def second(i, carry):
                row0 = pl.multiple_of(k * chunk + i * short_rows, short_rows)
                here = pl.ds(row0, short_rows)
                updated = asm[here, PANEL:BOTH] - dot_t(l_v[here, 0:PANEL], top_v[...])
                value = dot_exact(updated, inverse2[...]).astype(BF16)
                none = jnp.zeros_like(value)
                raw_v[here, PANEL:BOTH] = jnp.where(r * rows + row0 >= PANEL, value, none)
                l_v[here, PANEL:BOTH] = jnp.where(r * rows + row0 >= BOTH, value, none)
                return carry

            lax.fori_loop(0, chunk // short_rows, second, 0)
            for j in range(1, n_col):
                to_col(k, j).start()
            to_half(k, l_v).start()
            keep_rows(k).start()
            keep_raw(k).start()

            @pl.when(z == slab)
            def _():
                send_cols(k, l_v, None)

        @pl.when(r == 0)
        def _():
            for j in range(1, n_row):
                to_top(j).wait_send()

    def pass_rows(k):
        @pl.when(slab != 0)
        def _():
            to_half(k, lrows).wait_recv()

            @pl.when((h == 0) & (c != 0))
            def _():
                to_half(k, lrows).start()

            @pl.when(z == slab)
            def _():
                send_cols(k, lrows, None)

    def pass_cols(k):
        @pl.when(z != slab)
        def _():
            here = slot_part(lcols, k)
            to_line(k, 1, here).wait_recv()

            @pl.when((z > slab) & (z + 1 < n_z))
            def _():
                to_line(k, 1, here).start()

            @pl.when((z < slab) & (z >= 1))
            def _():
                to_line(k, -1, here).start()

            for d in range(1, fanout):
                to_lane(k, d, here).start()

    for step in range(CHUNKS + LAG):
        if step < CHUNKS:
            pass_rows(step)
        if step >= LAG:
            pass_cols(step - LAG)

    for k in range(CHUNKS):
        here = slot_part(lcols, k)
        for d in range(1, fanout):
            other = lax.rem(lane + fanout - d, fanout)
            landed = lcols.at[pl.ds(pl.multiple_of(other * rows + k * chunk, chunk), chunk), :]
            pltpu.make_async_remote_copy(
                src_ref=landed, dst_ref=landed, send_sem=lane_send.at[d, k],
                recv_sem=lane_recv.at[d, k], device_id={"half": 1 - h}, device_id_type=MESH_IDS,
            ).wait_recv()
            to_lane(k, d, here).wait_send()

        @pl.when(root)
        def _():
            for j in range(1, n_col):
                to_col(k, j).wait_send()
            keep_rows(k).wait()
            keep_raw(k).wait()

        @pl.when(h == 0)
        def _():
            to_half(k, lrows).wait_send()

        @pl.when((z >= slab) & (z + 1 < n_z))
        def _():
            to_line(k, 1, here).wait_send()

        @pl.when((z <= slab) & (z >= 1))
        def _():
            to_line(k, -1, here).wait_send()

        @pl.when(z == slab)
        def _():
            keep_cols(k, lrows).wait()

    @pl.when(slab == 1)
    def _():
        early.wait_send()

    late.wait()


def update_kernel(
    place, cmap, fill, front, own, other, lrows, lcols, raw, out, product
):
    half, slab, row_group0, col_group0 = place[0], place[1], place[2], place[3]
    j, i = pl.program_id(0), pl.program_id(1)
    tile_cols = front.shape[1]
    product[...] = dot_t(lrows[...], lcols[...])
    row_group = row_group0 + i
    pieces = ((half, own), (1 - half, other))
    row_spots = [[locate(cmap, source, row_group, p) for p in range(4)] for source, _ in pieces]
    for q in range(tile_cols // BLOCK):
        col_group = col_group0 + j * (tile_cols // BOTH) + q // 4
        col_spots = [locate(cmap, source, col_group, q % 4) for source, _ in pieces]
        columns = slice(q * BLOCK, (q + 1) * BLOCK)
        for p in range(4):
            here = slice(p * BLOCK, (p + 1) * BLOCK)
            total = front[here, columns].astype(F32)
            for n, (source, piece) in enumerate(pieces):
                kr, hit_r = row_spots[n][p]
                kc, hit_c = col_spots[n]
                use = hit_r & hit_c & (fill[source, 3 * row_group + kr, 3 * col_group + kc] != 0)
                block = piece[
                    pl.ds(pl.multiple_of(kr * BLOCK, BLOCK), BLOCK),
                    pl.ds(pl.multiple_of(q // 4 * GROUP + kc * BLOCK, BLOCK), BLOCK),
                ]
                total = total + jnp.where(use, block.astype(F32), 0.0)
            out[here, columns] = (total - product[here, columns]).astype(BF16)

    @pl.when((slab == 0) & (j == 0))
    def _():
        out[:, 0:BOTH] = raw[...]


def body(sizes, front_matrix, child_update, fill_pattern, child_map, first_inverse, second_inverse):
    n_half, n_row, n_col = sizes
    rows, width = front_matrix.shape[0], front_matrix.shape[3]
    front = front_matrix.reshape(rows, width)
    child = child_update.reshape(child_update.shape[1:])
    child_rows, half_width = child.shape[0], child.shape[1] // 2
    fanout = n_row // (2 * n_col)
    any_space = pl.BlockSpec(memory_space=pl.ANY)
    smem = pl.BlockSpec(memory_space=pltpu.SMEM)
    vmem = pl.BlockSpec(memory_space=pltpu.VMEM)
    dma = pltpu.SemaphoreType.DMA
    received, lrows, lcols, raw = pl.pallas_call(
        functools.partial(panel_kernel, n_half, n_row, n_col),
        out_shape=[
            jax.ShapeDtypeStruct((child_rows, half_width), BF16),
            jax.ShapeDtypeStruct((rows, BOTH), BF16),
            jax.ShapeDtypeStruct((width, BOTH), BF16),
            jax.ShapeDtypeStruct((rows, BOTH), BF16),
        ],
        in_specs=[any_space, any_space, smem, smem, vmem, vmem],
        out_specs=[any_space] * 4,
        scratch_shapes=[
            pltpu.VMEM((rows, BOTH), BF16),
            pltpu.VMEM((child_rows, GROUP), BF16),
            pltpu.VMEM((child_rows, GROUP), BF16),
            pltpu.VMEM((rows, BOTH), F32),
            pltpu.VMEM((rows, BOTH), BF16),
            pltpu.VMEM((rows, BOTH), BF16),
            pltpu.VMEM((PANEL, PANEL), BF16),
            dma((2,)), dma, dma, dma, dma, dma((n_row,)), dma,
            dma((n_col, CHUNKS)), dma((CHUNKS,)),
            dma((2, CHUNKS)), dma((CHUNKS,)),
            dma((fanout, CHUNKS)), dma((fanout, CHUNKS)), dma((3, CHUNKS)),
        ],
        compiler_params=pltpu.CompilerParams(
            collective_id=0, has_side_effects=True, vmem_limit_bytes=40 * 2**20
        ),
        name="panels",
    )(front, child, fill_pattern, child_map, first_inverse, second_inverse)

    half = lax.axis_index("half")
    row = lax.axis_index("row")
    slab = lax.axis_index("col") * 2 + half
    place = jnp.stack([half, slab, row * (rows // BOTH), slab * (width // BOTH)]).astype(jnp.int32)
    tile = 2 * BOTH
    tile_child = 2 * GROUP
    halves = half_width // tile_child
    out = pl.pallas_call(
        update_kernel,
        out_shape=jax.ShapeDtypeStruct((rows, width), BF16),
        grid_spec=pltpu.PrefetchScalarGridSpec(
            num_scalar_prefetch=3,
            grid=(width // tile, rows // BOTH),
            in_specs=[
                pl.BlockSpec((BOTH, tile), lambda j, i, *_: (i, j)),
                pl.BlockSpec((GROUP, tile_child), lambda j, i, place, *_: (i, place[0] * halves + j)),
                pl.BlockSpec((GROUP, tile_child), lambda j, i, *_: (i, j)),
                pl.BlockSpec((BOTH, BOTH), lambda j, i, *_: (i, 0)),
                pl.BlockSpec((tile, BOTH), lambda j, i, *_: (j, 0)),
                pl.BlockSpec((BOTH, BOTH), lambda j, i, *_: (i, 0)),
            ],
            out_specs=pl.BlockSpec((BOTH, tile), lambda j, i, *_: (i, j)),
            scratch_shapes=[pltpu.VMEM((BOTH, tile), F32)],
        ),
        compiler_params=pltpu.CompilerParams(vmem_limit_bytes=48 * 2**20),
        name="update",
    )(place, child_map, fill_pattern, front, child, received, lrows, lcols, raw)
    return out.reshape(rows, 1, 1, width)


def solution(mesh):
    placed = (P("row", "col", "half", None), P("half", "row", "col"), P(), P(), P(), P())
    sizes = (mesh.shape["half"], mesh.shape["row"], mesh.shape["col"])
    return jax.shard_map(
        functools.partial(body, sizes), mesh=mesh, in_specs=placed,
        out_specs=P("row", "col", "half", None), check_vma=False,
    )
```

```python
import functools

import jax
import jax.numpy as jnp
from jax import lax
from jax.experimental import pallas as pl
from jax.experimental.pallas import tpu as pltpu
from jax.sharding import PartitionSpec as P

BLOCK = 128
PANEL = 256
BOTH = 2 * PANEL
GROUP = 3 * BLOCK
CHUNKS = 16
LAG = 5
MESH_IDS = pl.DeviceIdType.MESH
F32 = jnp.float32
BF16 = jnp.bfloat16


def dot_t(a, b):
    return lax.dot_general(a, b, (((1,), (1,)), ((), ())), preferred_element_type=F32)


def dot_exact(a, b):
    high = a.astype(BF16)
    rest = a - high.astype(F32)
    mid = rest.astype(BF16)
    low = (rest - mid.astype(F32)).astype(BF16)
    return dot_t(low, b) + dot_t(mid, b) + dot_t(high, b)


def locate(cmap, source, group, slot):
    target = 4 * group + slot
    m0 = cmap[source, 3 * group]
    m1 = cmap[source, 3 * group + 1]
    m2 = cmap[source, 3 * group + 2]
    k = jnp.where(m1 <= target, 1, 0)
    k = jnp.where(m2 <= target, 2, k)
    hit = (m0 == target) | (m1 == target) | (m2 == target)
    return k, hit


def panel_kernel(
    n_half, n_row, n_col,
    front, child, fill, cmap, inverse1, inverse2,
    received, lrows, lcols, raw,
    front_v, own_v, other_v, asm, l_v, raw_v, top_v,
    load_sem, early_send, early_recv, late_send, late_recv, top_send, top_recv,
    row_send, row_recv, line_send, line_recv, lane_send, lane_recv, out_sem,
):
    rows = front.shape[0]
    half_width = received.shape[1]
    chunk = rows // CHUNKS
    fanout = n_row // (2 * n_col)
    n_z = n_row // fanout
    h, r, c = lax.axis_index("half"), lax.axis_index("row"), lax.axis_index("col")
    slab = 2 * c + h
    z, lane = lax.div(r, fanout), lax.rem(r, fanout)
    root = slab == 0

    barrier = pltpu.get_barrier_semaphore()
    pl.semaphore_signal(barrier, inc=1, device_id={"half": 1 - h}, device_id_type=MESH_IDS)
    for k in range(1, n_col):
        pl.semaphore_signal(
            barrier, inc=1, device_id={"col": lax.rem(c + k, n_col)}, device_id_type=MESH_IDS
        )
    for k in range(1, n_row):
        pl.semaphore_signal(
            barrier, inc=1, device_id={"row": lax.rem(r + k, n_row)}, device_id_type=MESH_IDS
        )
    load_front = pltpu.make_async_copy(front.at[:, pl.ds(0, BOTH)], front_v, load_sem.at[0])
    load_own = pltpu.make_async_copy(child.at[:, pl.ds(0, GROUP)], own_v, load_sem.at[1])

    @pl.when(root)
    def _():
        load_front.start()
        load_own.start()

    pl.semaphore_wait(barrier, 1 + (n_col - 1) + (n_row - 1))

    early = pltpu.make_async_remote_copy(
        src_ref=child.at[:, pl.ds(0, GROUP)], dst_ref=other_v,
        send_sem=early_send, recv_sem=early_recv,
        device_id={"half": 1 - h}, device_id_type=MESH_IDS,
    )
    start = pl.multiple_of((1 - h) * half_width, 128)
    late = pltpu.make_async_remote_copy(
        src_ref=child.at[:, pl.ds(start, half_width)], dst_ref=received,
        send_sem=late_send, recv_sem=late_recv,
        device_id={"half": 1 - h}, device_id_type=MESH_IDS,
    )

    @pl.when(slab == 1)
    def _():
        early.start()

    late.start()

    def part(ref, k):
        return ref.at[pl.ds(k * chunk, chunk), :]

    def slot_part(ref, k):
        return ref.at[pl.ds(pl.multiple_of(lane * rows + k * chunk, chunk), chunk), :]

    def to_col(k, j):
        return pltpu.make_async_remote_copy(
            src_ref=part(l_v, k), dst_ref=part(lrows, k),
            send_sem=row_send.at[j, k], recv_sem=row_recv.at[k],
            device_id={"col": j}, device_id_type=MESH_IDS,
        )

    def to_half(k, src):
        return pltpu.make_async_remote_copy(
            src_ref=part(src, k), dst_ref=part(lrows, k),
            send_sem=row_send.at[0, k], recv_sem=row_recv.at[k],
            device_id={"half": 1 - h}, device_id_type=MESH_IDS,
        )

    def to_line(k, step, src):
        return pltpu.make_async_remote_copy(
            src_ref=src, dst_ref=slot_part(lcols, k),
            send_sem=line_send.at[(step + 1) // 2, k], recv_sem=line_recv.at[k],
            device_id={"row": r + step * fanout}, device_id_type=MESH_IDS,
        )

    def to_lane(k, d, src):
        return pltpu.make_async_remote_copy(
            src_ref=src, dst_ref=slot_part(lcols, k),
            send_sem=lane_send.at[d, k], recv_sem=lane_recv.at[d, k],
            device_id={"row": z * fanout + lax.rem(lane + d, fanout)}, device_id_type=MESH_IDS,
        )

    def keep_rows(k):
        return pltpu.make_async_copy(part(l_v, k), part(lrows, k), out_sem.at[0, k])

    def keep_raw(k):
        return pltpu.make_async_copy(part(raw_v, k), part(raw, k), out_sem.at[1, k])

    def keep_cols(k, src):
        return pltpu.make_async_copy(part(src, k), slot_part(lcols, k), out_sem.at[2, k])

    def send_cols(k, src, src_slot):
        @pl.when(z + 1 < n_z)
        def _():
            to_line(k, 1, part(src, k)).start()

        @pl.when(z >= 1)
        def _():
            to_line(k, -1, part(src, k)).start()

        for d in range(1, fanout):
            to_lane(k, d, part(src, k)).start()
        keep_cols(k, src).start()

    @pl.when(root)
    def _():
        load_front.wait()
        load_own.wait()
        early.wait_recv()
        groups = rows // BOTH

        def lands(source, index, target):
            apart = cmap[source, index] - target
            return 1 - jnp.minimum(apart * apart, 1)

        def assemble(g, carry):
            group = r * groups + g
            for t in range(4):
                row0 = pl.multiple_of(g * BOTH + t * BLOCK, BLOCK)
                for q in range(4):
                    total = front_v[pl.ds(row0, BLOCK), q * BLOCK : (q + 1) * BLOCK].astype(F32)
                    for source, piece in ((0, own_v), (1, other_v)):
                        for kr in range(max(t - 1, 0), min(t, 2) + 1):
                            hit_r = lands(source, 3 * group + kr, 4 * group + t)
                            for kc in range(max(q - 1, 0), min(q, 2) + 1):
                                hit = hit_r * lands(source, kc, q) * fill[source, 3 * group + kr, kc]
                                block = piece[
                                    pl.ds(pl.multiple_of(g * GROUP + kr * BLOCK, BLOCK), BLOCK),
                                    kc * BLOCK : (kc + 1) * BLOCK,
                                ]
                                total = total + block.astype(F32) * hit.astype(F32)
                    asm[pl.ds(row0, BLOCK), q * BLOCK : (q + 1) * BLOCK] = total
            return carry

        lax.fori_loop(0, groups, assemble, 0)

        step_rows = PANEL

        def first(k, carry):
            row0 = pl.multiple_of(k * step_rows, step_rows)
            value = dot_exact(asm[pl.ds(row0, step_rows), 0:PANEL], inverse1[...]).astype(BF16)
            raw_v[pl.ds(row0, step_rows), 0:PANEL] = value
            keep = r * rows + row0 >= PANEL
            l_v[pl.ds(row0, step_rows), 0:PANEL] = jnp.where(keep, value, jnp.zeros_like(value))
            return carry

        lax.fori_loop(0, rows // step_rows, first, 0)

        def to_top(j):
            return pltpu.make_async_remote_copy(
                src_ref=top_v, dst_ref=top_v, send_sem=top_send.at[j], recv_sem=top_recv,
                device_id={"row": j}, device_id_type=MESH_IDS,
            )

        @pl.when(r == 0)
        def _():
            top_v[...] = raw_v[PANEL:BOTH, 0:PANEL]
            for j in range(1, n_row):
                to_top(j).start()

        @pl.when(r != 0)
        def _():
            to_top(0).wait_recv()

        span = max(PANEL, chunk)
        for k in range(CHUNKS):

            def second(i, carry):
                row0 = pl.multiple_of(k * chunk + i * step_rows, step_rows)
                here = pl.ds(row0, step_rows)
                updated = asm[here, PANEL:BOTH] - dot_t(l_v[here, 0:PANEL], top_v[...])
                value = dot_exact(updated, inverse2[...]).astype(BF16)
                none = jnp.zeros_like(value)
                raw_v[here, PANEL:BOTH] = jnp.where(r * rows + row0 >= PANEL, value, none)
                l_v[here, PANEL:BOTH] = jnp.where(r * rows + row0 >= BOTH, value, none)
                return carry

            if k * chunk % span == 0:
                lax.fori_loop(0, span // step_rows, second, 0)
            for j in range(1, n_col):
                to_col(k, j).start()
            to_half(k, l_v).start()
            keep_rows(k).start()
            keep_raw(k).start()

            @pl.when(z == slab)
            def _():
                send_cols(k, l_v, None)

        @pl.when(r == 0)
        def _():
            for j in range(1, n_row):
                to_top(j).wait_send()

    def pass_rows(k):
        @pl.when(slab != 0)
        def _():
            to_half(k, lrows).wait_recv()

            @pl.when((h == 0) & (c != 0))
            def _():
                to_half(k, lrows).start()

            @pl.when(z == slab)
            def _():
                send_cols(k, lrows, None)

    def pass_cols(k):
        @pl.when(z != slab)
        def _():
            here = slot_part(lcols, k)
            to_line(k, 1, here).wait_recv()

            @pl.when((z > slab) & (z + 1 < n_z))
            def _():
                to_line(k, 1, here).start()

            @pl.when((z < slab) & (z >= 1))
            def _():
                to_line(k, -1, here).start()

            for d in range(1, fanout):
                to_lane(k, d, here).start()

    for step in range(CHUNKS + LAG):
        if step < CHUNKS:
            pass_rows(step)
        if step >= LAG:
            pass_cols(step - LAG)

    for k in range(CHUNKS):
        here = slot_part(lcols, k)
        for d in range(1, fanout):
            other = lax.rem(lane + fanout - d, fanout)
            landed = lcols.at[pl.ds(pl.multiple_of(other * rows + k * chunk, chunk), chunk), :]
            pltpu.make_async_remote_copy(
                src_ref=landed, dst_ref=landed, send_sem=lane_send.at[d, k],
                recv_sem=lane_recv.at[d, k], device_id={"half": 1 - h}, device_id_type=MESH_IDS,
            ).wait_recv()
            to_lane(k, d, here).wait_send()

        @pl.when(root)
        def _():
            for j in range(1, n_col):
                to_col(k, j).wait_send()
            keep_rows(k).wait()
            keep_raw(k).wait()

        @pl.when(h == 0)
        def _():
            to_half(k, lrows).wait_send()

        @pl.when((z >= slab) & (z + 1 < n_z))
        def _():
            to_line(k, 1, here).wait_send()

        @pl.when((z <= slab) & (z >= 1))
        def _():
            to_line(k, -1, here).wait_send()

        @pl.when(z == slab)
        def _():
            keep_cols(k, lrows).wait()

    @pl.when(slab == 1)
    def _():
        early.wait_send()

    late.wait()


def update_kernel(
    place, cmap, fill, front, own, other, lrows, lcols, raw, out, product
):
    half, slab, row_group0, col_group0 = place[0], place[1], place[2], place[3]
    j, i = pl.program_id(0), pl.program_id(1)
    tile_cols = front.shape[1]
    product[...] = dot_t(lrows[...], lcols[...])
    row_group = row_group0 + i
    pieces = ((half, own), (1 - half, other))
    row_spots = [[locate(cmap, source, row_group, p) for p in range(4)] for source, _ in pieces]
    for q in range(tile_cols // BLOCK):
        col_group = col_group0 + j * (tile_cols // BOTH) + q // 4
        col_spots = [locate(cmap, source, col_group, q % 4) for source, _ in pieces]
        columns = slice(q * BLOCK, (q + 1) * BLOCK)
        for p in range(4):
            here = slice(p * BLOCK, (p + 1) * BLOCK)
            total = front[here, columns].astype(F32)
            for n, (source, piece) in enumerate(pieces):
                kr, hit_r = row_spots[n][p]
                kc, hit_c = col_spots[n]
                use = hit_r & hit_c & (fill[source, 3 * row_group + kr, 3 * col_group + kc] != 0)
                block = piece[
                    pl.ds(pl.multiple_of(kr * BLOCK, BLOCK), BLOCK),
                    pl.ds(pl.multiple_of(q // 4 * GROUP + kc * BLOCK, BLOCK), BLOCK),
                ]
                total = total + jnp.where(use, block.astype(F32), 0.0)
            out[here, columns] = (total - product[here, columns]).astype(BF16)

    @pl.when((slab == 0) & (j == 0))
    def _():
        out[:, 0:BOTH] = raw[...]


def body(sizes, front_matrix, child_update, fill_pattern, child_map, first_inverse, second_inverse):
    n_half, n_row, n_col = sizes
    rows, width = front_matrix.shape[0], front_matrix.shape[3]
    front = front_matrix.reshape(rows, width)
    child = child_update.reshape(child_update.shape[1:])
    child_rows, half_width = child.shape[0], child.shape[1] // 2
    fanout = n_row // (2 * n_col)
    any_space = pl.BlockSpec(memory_space=pl.ANY)
    smem = pl.BlockSpec(memory_space=pltpu.SMEM)
    vmem = pl.BlockSpec(memory_space=pltpu.VMEM)
    dma = pltpu.SemaphoreType.DMA
    received, lrows, lcols, raw = pl.pallas_call(
        functools.partial(panel_kernel, n_half, n_row, n_col),
        out_shape=[
            jax.ShapeDtypeStruct((child_rows, half_width), BF16),
            jax.ShapeDtypeStruct((rows, BOTH), BF16),
            jax.ShapeDtypeStruct((width, BOTH), BF16),
            jax.ShapeDtypeStruct((rows, BOTH), BF16),
        ],
        in_specs=[any_space, any_space, smem, smem, vmem, vmem],
        out_specs=[any_space] * 4,
        scratch_shapes=[
            pltpu.VMEM((rows, BOTH), BF16),
            pltpu.VMEM((child_rows, GROUP), BF16),
            pltpu.VMEM((child_rows, GROUP), BF16),
            pltpu.VMEM((rows, BOTH), F32),
            pltpu.VMEM((rows, BOTH), BF16),
            pltpu.VMEM((rows, BOTH), BF16),
            pltpu.VMEM((PANEL, PANEL), BF16),
            dma((2,)), dma, dma, dma, dma, dma((n_row,)), dma,
            dma((n_col, CHUNKS)), dma((CHUNKS,)),
            dma((2, CHUNKS)), dma((CHUNKS,)),
            dma((fanout, CHUNKS)), dma((fanout, CHUNKS)), dma((3, CHUNKS)),
        ],
        compiler_params=pltpu.CompilerParams(
            collective_id=0, has_side_effects=True, vmem_limit_bytes=40 * 2**20
        ),
        name="panels",
    )(front, child, fill_pattern, child_map, first_inverse, second_inverse)

    half = lax.axis_index("half")
    row = lax.axis_index("row")
    slab = lax.axis_index("col") * 2 + half
    place = jnp.stack([half, slab, row * (rows // BOTH), slab * (width // BOTH)]).astype(jnp.int32)
    tile = 2 * BOTH
    tile_child = 2 * GROUP
    halves = half_width // tile_child
    out = pl.pallas_call(
        update_kernel,
        out_shape=jax.ShapeDtypeStruct((rows, width), BF16),
        grid_spec=pltpu.PrefetchScalarGridSpec(
            num_scalar_prefetch=3,
            grid=(width // tile, rows // BOTH),
            in_specs=[
                pl.BlockSpec((BOTH, tile), lambda j, i, *_: (i, j)),
                pl.BlockSpec((GROUP, tile_child), lambda j, i, place, *_: (i, place[0] * halves + j)),
                pl.BlockSpec((GROUP, tile_child), lambda j, i, *_: (i, j)),
                pl.BlockSpec((BOTH, BOTH), lambda j, i, *_: (i, 0)),
                pl.BlockSpec((tile, BOTH), lambda j, i, *_: (j, 0)),
                pl.BlockSpec((BOTH, BOTH), lambda j, i, *_: (i, 0)),
            ],
            out_specs=pl.BlockSpec((BOTH, tile), lambda j, i, *_: (i, j)),
            scratch_shapes=[pltpu.VMEM((BOTH, tile), F32)],
        ),
        compiler_params=pltpu.CompilerParams(vmem_limit_bytes=48 * 2**20),
        name="update",
    )(place, child_map, fill_pattern, front, child, received, lrows, lcols, raw)
    return out.reshape(rows, 1, 1, width)


def solution(mesh):
    placed = (P("row", "col", "half", None), P("half", "row", "col"), P(), P(), P(), P())
    sizes = (mesh.shape["half"], mesh.shape["row"], mesh.shape["col"])
    return jax.shard_map(
        functools.partial(body, sizes), mesh=mesh, in_specs=placed,
        out_specs=P("row", "col", "half", None), check_vma=False,
    )
```
